32 devices in a mesh: energy: 4 (over z), cluster: 2 (over x), tile: 4 (over y, core).
Axes of the slice: x: 2, y: 2, z: 4, core: 2. Of those that a mesh axis runs over, the one named last changes fastest.
Arguments:
- boundary: bfloat16 [2, 2, 512, 8, 2, 1024], P('cluster', None, 'tile', 'energy'), may hold values from -5 to 5
- column_source: int32 [2, 1024], P('cluster'), may hold values from 0 to 1023, as said below
- energy_weights: float32 [8], P('energy'), may hold values from 0.2 to 2
Outputs:
- final_rows: float32 [2, 512, 8, 2, 1024], P('cluster', 'tile', 'energy')
- density: float32 [2, 512], P('cluster', 'tile')
The draws below stay inside these ranges and needn't reach their ends.
Inputs may be any that keep to these rules, and one draw needn't show every extreme that they name: `column_source`: for each cluster, every index 0 to 1023 appears once.
All inputs are finite; a program needn't handle non-finite values.
Results may differ from the reference program's by a relative error of at most 0.015.
Values may be sent and summed in bfloat16 or wider, within the bound.
A program may use at most 64 MiB of HBM per device.

```python
import math
import jax
import jax.numpy as jnp
from jax import lax

S = 512
B = 1024
NE = 8
NC = 2
LEVELS = 1
ROWS = 128
OUT_ROWS = 512


def shared_order(key):
    keys = jax.random.split(jax.random.fold_in(key, 11), NC)
    return jax.vmap(lambda single_key: jax.random.permutation(single_key, B))(keys).astype(jnp.int32)


def draw_column_source(key, part):
    return shared_order(key)


def draw_boundary(key, part):
    order = shared_order(key)
    shape = (NC, 2, S, NE, 2, B)
    keys = jax.random.split(jax.random.fold_in(key, 23), 3)
    couple_scale = 0.9 * S ** (-0.25)
    node_of_column = jax.vmap(lambda single_order: jnp.zeros((B,), jnp.int32).at[single_order].set(jnp.arange(B, dtype=jnp.int32)))(order)
    column_outer = (node_of_column >= S)[:, None, None, None, None, :]
    row_outer = (jnp.arange(2) == 1)[None, :, None, None, None, None]
    coupled = column_outer != row_outer
    base = jax.random.truncated_normal(keys[0], -3.0, 3.0, shape, jnp.float32)
    diag_real = jax.random.uniform(keys[1], (NC, 2, S, NE), jnp.float32, 2.0, 4.0)
    diag_imag = jax.random.uniform(keys[2], (NC, 2, S, NE), jnp.float32, 0.2, 1.0)
    noise = base * jnp.where(coupled, couple_scale, 0.04)
    target = order.reshape(NC, 2, S)
    hitting = (jnp.arange(B)[None, None, None, :] == target[:, :, :, None])[:, :, :, None, None, :]
    diagonal = jnp.stack([diag_real, diag_imag], axis=4)[..., None]
    return (noise + jnp.where(hitting, diagonal, 0.0)).astype(jnp.bfloat16)


def level_of(rng, shape, cuts, smallest, largest):
    gain = 1.0
    for axis_at, shards_of in cuts:
        heights = jax.random.uniform(jax.random.fold_in(jax.random.fold_in(rng, 6), axis_at), (shards_of,), jnp.float32, smallest / len(cuts), largest / len(cuts))
        gain = gain * jnp.repeat(jnp.exp(heights), shape[axis_at] // shards_of).reshape((-1,) + (1,) * (len(shape) - 1 - axis_at))
    return gain


def setup_inputs(seed: int = 0) -> dict:
    streams_of = jax.random.split(jax.random.key(seed), 4)
    boundary = draw_boundary(jax.random.fold_in(streams_of[3], 71), 0)
    column_source = draw_column_source(jax.random.fold_in(streams_of[3], 71), 0)
    energy_weights = jnp.clip(jnp.exp(math.log(2.0) - 2.3025851 * jax.random.uniform(streams_of[2], (NE,), jnp.float32) ** level_of(streams_of[2], (NE,), ((0, 4),), -0.2, 0.2)), 0.2, 2.0)
    return dict(boundary=boundary, column_source=column_source, energy_weights=energy_weights)


def complex_dot(left, right):
    real_part = jnp.dot(left[0], right[0], preferred_element_type=jnp.float32) - jnp.dot(left[1], right[1], preferred_element_type=jnp.float32)
    imag_part = jnp.dot(left[0], right[1], preferred_element_type=jnp.float32) + jnp.dot(left[1], right[0], preferred_element_type=jnp.float32)
    return jnp.stack([real_part, imag_part])


def inverse_guess(interior):
    values = interior.astype(jnp.float32)
    diag_real = jnp.diagonal(values[0])
    diag_imag = jnp.diagonal(values[1])
    denom = diag_real * diag_real + diag_imag * diag_imag
    inv_real = diag_real / denom
    inv_imag = -diag_imag / denom
    temp_real = values[0] * inv_real[None, :] - values[1] * inv_imag[None, :]
    temp_imag = values[0] * inv_imag[None, :] + values[1] * inv_real[None, :]
    prod_real = inv_real[:, None] * temp_real - inv_imag[:, None] * temp_imag
    prod_imag = inv_real[:, None] * temp_imag + inv_imag[:, None] * temp_real
    ident = jnp.eye(values.shape[1], dtype=jnp.float32)
    guess_real = 2.0 * ident * inv_real[:, None] - prod_real
    guess_imag = 2.0 * ident * inv_imag[:, None] - prod_imag
    return jnp.stack([guess_real, guess_imag]).astype(jnp.bfloat16)


def merge_pair(low, high):
    interior = (low[:, :S, :S] + high[:, :S, :S]).astype(jnp.bfloat16)
    approx_inverse = inverse_guess(interior)
    left = jnp.concatenate([low[:, S:, :S], high[:, S:, :S]], axis=1).astype(jnp.bfloat16)
    right = jnp.concatenate([low[:, :S, S:], high[:, :S, S:]], axis=2).astype(jnp.bfloat16)
    applied = complex_dot(left, approx_inverse)
    middle = complex_dot(applied.astype(jnp.bfloat16), interior).astype(jnp.bfloat16)
    reduced = (2.0 * applied - complex_dot(middle, approx_inverse)).astype(jnp.bfloat16)
    zeros = jnp.zeros_like(low[:, S:, S:])
    upper = jnp.concatenate([low[:, S:, S:], zeros], axis=2)
    lower = jnp.concatenate([zeros, high[:, S:, S:]], axis=2)
    start = jnp.concatenate([upper, lower], axis=1)
    return start - complex_dot(reduced, right)


def reference(boundary, column_source, energy_weights):
    clusters = jnp.arange(NC).astype(jnp.int32)
    group = clusters // (2 ** LEVELS)
    side_bit = (clusters // (2 ** (LEVELS - 1))) % 2
    within = clusters % (2 ** (LEVELS - 1))
    quarter = ROWS // (2 ** (LEVELS - 1))
    index = jnp.arange(OUT_ROWS).astype(jnp.int32)
    rows = side_bit[:, None] * S + (index[None, :] // quarter) * ROWS + within[:, None] * quarter + index[None, :] % quarter

    def energy_step(energy):
        stored = lax.dynamic_index_in_dim(boundary, energy, 3, keepdims=False)
        canonical = jnp.take_along_axis(stored, column_source[:, None, None, None, :], axis=4)
        blocks = canonical.reshape(NC, B, 2, B).transpose(0, 2, 1, 3).astype(jnp.float32)
        for level_index in range(LEVELS):
            paired = blocks.reshape(-1, 2, 2, B, B)
            blocks = jax.vmap(merge_pair)(paired[:, 0], paired[:, 1])
        picked = blocks[group[:, None], :, rows, :]
        diagonal = blocks[group[:, None], 1, rows, rows]
        return picked, diagonal

    picked, diagonal = lax.map(energy_step, jnp.arange(NE).astype(jnp.int32))
    final_rows = picked.transpose(1, 2, 0, 3, 4)
    density = jnp.sum(energy_weights[:, None, None] * diagonal, axis=0)
    return final_rows, density
```

```python
import functools

import jax
import jax.numpy as jnp
from jax import lax
from jax.experimental import pallas as pl
from jax.experimental.pallas import tpu as pltpu
from jax.sharding import PartitionSpec as P


def swapped(shard, axis, distance):
    return lax.ppermute(shard, axis, [(i, i ^ 1 << distance) for i in range(lax.axis_size(axis))])


def shortened(shard):
    return jax.tree.map(lambda a: a.astype(jnp.bfloat16) if a.dtype == jnp.float32 else a, shard)


def complex_product(left, right):

    def single(first_part, second_part):
        return jnp.einsum(
            "mek,ken->men", first_part, second_part, preferred_element_type=jnp.float32
        )

    real_part = single(left[:, :, 0], right[:, :, 0]) - single(left[:, :, 1], right[:, :, 1])
    imag_part = single(left[:, :, 0], right[:, :, 1]) + single(left[:, :, 1], right[:, :, 0])
    return jnp.stack([real_part, imag_part], axis=2)


def inverse_guess(interior):
    values = interior.astype(jnp.float32)
    same = jnp.eye(values.shape[0], dtype=jnp.float32)[:, None, None, :]
    diagonal = jnp.sum(values * same, axis=0)
    denom = diagonal[:, 0] * diagonal[:, 0] + diagonal[:, 1] * diagonal[:, 1]
    inv_real = diagonal[:, 0] / denom
    inv_imag = -diagonal[:, 1] / denom
    column_real = inv_real[None, :, :]
    column_imag = inv_imag[None, :, :]
    row_real = inv_real.T[:, :, None]
    row_imag = inv_imag.T[:, :, None]
    values_real = values[:, :, 0]
    values_imag = values[:, :, 1]
    temp_real = values_real * column_real - values_imag * column_imag
    temp_imag = values_real * column_imag + values_imag * column_real
    prod_real = row_real * temp_real - row_imag * temp_imag
    prod_imag = row_real * temp_imag + row_imag * temp_real
    ident = jnp.eye(values.shape[0], dtype=jnp.float32)[:, None, :]
    guess_real = 2.0 * ident * row_real - prod_real
    guess_imag = 2.0 * ident * row_imag - prod_imag
    return jnp.stack([guess_real, guess_imag], axis=2).astype(jnp.bfloat16)


def place_block(block, is_low):
    zeros = jnp.zeros_like(block)
    return jnp.where(
        is_low, jnp.concatenate([block, zeros], axis=3), jnp.concatenate([zeros, block], axis=3)
    )


def swap_separator(separator, level_index):
    return swapped(separator, "cluster", level_index)


def eliminate(outer_coupling, start_block, interior, approx_inverse, coupling_rows):
    applied = complex_product(outer_coupling.astype(jnp.bfloat16), approx_inverse)
    middle = complex_product(applied.astype(jnp.bfloat16), interior).astype(jnp.bfloat16)
    reduced = (2.0 * applied - complex_product(middle, approx_inverse)).astype(jnp.bfloat16)
    row_piece = lax.all_gather(coupling_rows, "tile", axis=0, tiled=True)
    columns = lax.slice_in_dim(reduced, 0, row_piece.shape[0], axis=3)
    return start_block - complex_product(columns, row_piece)


def permuted(stored, source):
    nodes = jnp.arange(stored.shape[-1], dtype=jnp.int32)
    picks = (nodes[:, None] == source[None, :]).astype(jnp.bfloat16)
    picked = jnp.einsum("...j,jm->...m", stored, picks, preferred_element_type=jnp.float32)
    return picked.astype(jnp.bfloat16)


def per_device(boundary, column_source, energy_weights):
    stored = boundary[0]
    canonical = permuted(stored, column_source[0])
    separator = canonical[0]
    outer_rows = canonical[1]
    interior_width = separator.shape[3] // 2
    row_count = separator.shape[0]
    levels = min(2, lax.axis_size("cluster") // 2)
    cluster_index = lax.axis_index("cluster")
    tile_index = lax.axis_index("tile")
    for level_index in range(levels):
        side_bit = cluster_index // 2**level_index % 2
        is_low = side_bit == 0
        final_level = level_index == levels - 1
        if final_level:
            separator = separator.astype(jnp.float32)
            outer_rows = outer_rows.astype(jnp.float32)
            partner_outer = outer_rows
            partner_sep = swap_separator(separator, level_index)
        else:
            partner_sep, partner_outer = (
                swapped(shortened(separator), "cluster", level_index).astype(separator.dtype),
                swapped(shortened(outer_rows), "cluster", level_index).astype(outer_rows.dtype),
            )
            separator = separator.astype(jnp.float32)
            outer_rows = outer_rows.astype(jnp.float32)
            partner_sep = partner_sep.astype(jnp.float32)
            partner_outer = partner_outer.astype(jnp.float32)
        interior_rows = (
            separator[..., :interior_width] + partner_sep[..., :interior_width]
        ).astype(jnp.bfloat16)
        interior = lax.all_gather(interior_rows, "tile", axis=0, tiled=True)
        approx_inverse = inverse_guess(interior)
        low_sep = jnp.where(is_low, separator, partner_sep)
        high_sep = jnp.where(is_low, partner_sep, separator)
        coupling_rows = jnp.concatenate(
            [low_sep[..., interior_width:], high_sep[..., interior_width:]], axis=3
        ).astype(jnp.bfloat16)
        if final_level:
            share = row_count // 2**level_index
            within = cluster_index % 2**level_index
            own_rows = lax.dynamic_slice_in_dim(outer_rows, within * share, share, 0)
            new_rows = eliminate(
                own_rows[..., :interior_width],
                place_block(own_rows[..., interior_width:], is_low),
                interior,
                approx_inverse,
                coupling_rows,
            )
            columns = (
                side_bit * interior_width
                + tile_index * row_count
                + within * share
                + jnp.arange(share, dtype=jnp.int32)
            )
            selector = (
                jnp.arange(new_rows.shape[3], dtype=jnp.int32)[None, :] == columns[:, None]
            ).astype(jnp.float32)
            diagonal = jnp.sum(new_rows[:, :, 1, :] * selector[:, None, :], axis=2)
            partial_sum = jnp.sum(diagonal * energy_weights[None, :], axis=1)
            density = lax.psum(partial_sum, "energy")
            return (new_rows[None], density[None])
        else:
            low_outer = jnp.where(is_low, outer_rows, partner_outer)
            high_outer = jnp.where(is_low, partner_outer, outer_rows)
            outer_coupling = jnp.concatenate(
                [low_outer[..., :interior_width], high_outer[..., :interior_width]], axis=0
            )
            start_block = jnp.concatenate(
                [
                    place_block(low_outer[..., interior_width:], True),
                    place_block(high_outer[..., interior_width:], False),
                ],
                axis=0,
            )
            merged = eliminate(outer_coupling, start_block, interior, approx_inverse, coupling_rows)
            separator = merged[:row_count]
            outer_rows = merged[row_count:]


LANES = 128


def dot(first, second):
    return jnp.dot(first, second, preferred_element_type=jnp.float32)


def complex_rows(stacked, real, imag):
    rows = stacked.shape[0] // 2
    by_real, by_imag = dot(stacked, real), dot(stacked, imag)
    return by_real[:rows] - by_imag[rows:], by_imag[:rows] + by_real[rows:]


def stack_rows(real, imag):
    return jnp.concatenate([real.astype(jnp.bfloat16), imag.astype(jnp.bfloat16)], axis=0)


def guess_of(real, imag):
    size = real.shape[0]
    step = min(128, size)
    ident = (
        lax.broadcasted_iota(jnp.int32, (step, step), 0)
        == lax.broadcasted_iota(jnp.int32, (step, step), 1)
    )

    def inverse_of(axis):
        def diagonal(values):
            cuts = [
                jnp.sum(
                    jnp.where(ident, values[b : b + step, b : b + step], 0.0),
                    axis=axis,
                    keepdims=True,
                )
                for b in range(0, size, step)
            ]
            return jnp.concatenate(cuts, axis=1 - axis)

        diag_real, diag_imag = diagonal(real), diagonal(imag)
        denom = diag_real * diag_real + diag_imag * diag_imag
        return diag_real / denom, -diag_imag / denom

    column_real, column_imag = inverse_of(0)
    row_real, row_imag = inverse_of(1)
    temp_real = real * column_real - imag * column_imag
    temp_imag = real * column_imag + imag * column_real
    prod_real = row_real * temp_real - row_imag * temp_imag
    prod_imag = row_real * temp_imag + row_imag * temp_real
    whole = (
        lax.broadcasted_iota(jnp.int32, real.shape, 0)
        == lax.broadcasted_iota(jnp.int32, real.shape, 1)
    )
    guess_real = jnp.where(whole, 2.0 * row_real, 0.0) - prod_real
    guess_imag = jnp.where(whole, 2.0 * row_imag, 0.0) - prod_imag
    return guess_real.astype(jnp.bfloat16), guess_imag.astype(jnp.bfloat16)


def merge_kernel(
    n_energy,
    boundary,
    source,
    weights,
    out,
    density,
    raw,
    picks,
    flat,
    outer,
    own_sep,
    peer_sep,
    inner,
    right,
    inverse,
    columns,
    terms,
    load_sem,
    store_sem,
    send_sem,
    recv_sem,
    term_send,
    term_recv,
):
    _, rows, energies, _, width = boundary.shape
    half = width // 2
    lines = rows * energies * 2
    every = energies * 2
    blocks = half // LANES

    def put(buffer, value, first=0):
        for block in range(blocks):
            buffer[first + block] = value[:, block * LANES : (block + 1) * LANES]

    def get(buffer, e, part, first=0):
        line = pl.ds(2 * e + part, rows, stride=every)
        return jnp.concatenate([buffer[first + b, line, :] for b in range(blocks)], axis=1)

    def scatter(buffer, e, part, value):
        line = pl.ds(2 * e + part, rows, stride=every)
        for block in range(blocks):
            buffer[block, line, :] = value[:, block * LANES : (block + 1) * LANES]

    cluster = lax.axis_index("cluster")
    tile = lax.axis_index("tile")
    energy = lax.axis_index("energy")
    over = 1 - cluster
    core = lax.rem(tile, 2)
    level = tile // 2
    beside = level * 2 + (1 - core)
    across = (1 - level) * 2 + core
    to_x, to_y, to_core = {"cluster": over}, {"tile": across}, {"tile": beside}

    loads = [
        pltpu.make_async_copy(
            boundary.at[part].reshape(lines, width), raw.at[part], load_sem.at[part]
        )
        for part in range(2)
    ]
    for load in loads:
        load.start()
    barrier = pltpu.get_barrier_semaphore()
    for there in (to_x, to_y, to_core):
        pl.semaphore_signal(barrier, inc=1, device_id=there, device_id_type=pl.DeviceIdType.MESH)
    for step in range(1, n_energy):
        pl.semaphore_signal(
            barrier,
            inc=1,
            device_id={"energy": lax.rem(energy + step, n_energy)},
            device_id_type=pl.DeviceIdType.MESH,
        )

    wanted = source[...]
    deep = min(256, width)
    for begin in range(0, width, deep):
        node = lax.broadcasted_iota(jnp.int32, (deep, width), 0) + begin
        picks[begin : begin + deep, :] = jnp.where(node == wanted, 1.0, 0.0).astype(jnp.bfloat16)
    loads[0].wait()
    pl.semaphore_wait(barrier, 2 + n_energy)

    def rows_of(which):
        return pl.ds(pl.multiple_of(which * rows, rows), rows)

    def send(kind, e, src, dst, there):
        copy = pltpu.make_async_remote_copy(
            src_ref=src,
            dst_ref=dst,
            send_sem=send_sem.at[kind, e],
            recv_sem=recv_sem.at[kind, e],
            device_id=there,
            device_id_type=pl.DeviceIdType.MESH,
        )
        copy.start()
        copies[kind, e] = copy

    def pass_on(kind, e, ref, there):
        send(kind, e, ref, ref, there)

    def right_at(which, e, block):
        return right.at[which, e, :, rows_of(block), :]

    def inner_at(e, block):
        return inner.at[e, :, rows_of(block), :]

    copies = {}
    sep_x, so_x, so_y, in_y, diag = range(5)
    core_in, core_in_y, core_so, core_so_y, core_so_x, core_diag = range(5, 11)
    all_e = list(range(energies))
    by_x = energies // 2

    put(flat, dot(raw[0], picks[:, :half]))
    for e in all_e:
        for part in range(2):
            own_sep[e, part] = get(flat, e, part).astype(jnp.bfloat16)
        send(sep_x, e, own_sep.at[e], peer_sep.at[e], to_x)
    put(flat, dot(raw[0], picks[:, half:]))
    for e in all_e:
        for part in range(2):
            right[cluster, e, part, rows_of(tile), :] = get(flat, e, part).astype(jnp.bfloat16)
        pass_on(so_y, e, right_at(cluster, e, tile), to_y)
    for e in reversed(all_e):
        pass_on(so_x, e, right_at(cluster, e, tile), to_x)
    for e in all_e:
        pass_on(core_so, e, right_at(cluster, e, tile), to_core)

    loads[1].wait()
    put(outer, dot(raw[1], picks[:, :half]))
    put(outer, dot(raw[1], picks[:, half:]), blocks)

    for e in all_e:
        copies[sep_x, e].wait_recv()
        for part in range(2):
            inner[e, part, rows_of(tile), :] = (
                own_sep[e, part].astype(jnp.float32) + peer_sep[e, part].astype(jnp.float32)
            ).astype(jnp.bfloat16)
        pass_on(in_y, e, inner_at(e, tile), to_y)
        pass_on(core_in, e, inner_at(e, tile), to_core)
        copies[so_y, e].wait_recv()
        if e < by_x:
            pass_on(diag, e, right_at(cluster, e, across), to_x)
        pass_on(core_so_y, e, right_at(cluster, e, across), to_core)

    def take_x(e):
        copies[so_x, e].wait_recv()
        if e >= by_x:
            pass_on(diag, e, right_at(over, e, tile), to_y)
        pass_on(core_so_x, e, right_at(over, e, tile), to_core)

    def take_inner(e):
        copies[in_y, e].wait_recv()
        pass_on(core_in_y, e, inner_at(e, across), to_core)

    for e, x in zip(all_e, reversed(all_e)):
        take_inner(e)
        take_x(x)
        copies[core_in, e].wait_recv()
        copies[core_in_y, e].wait_recv()
        guess_real, guess_imag = guess_of(
            inner[e, 0].astype(jnp.float32), inner[e, 1].astype(jnp.float32)
        )
        inverse[0] = guess_real
        inverse[1] = guess_imag
        left = stack_rows(get(outer, e, 0), get(outer, e, 1))
        applied_real, applied_imag = complex_rows(left, inverse[0], inverse[1])
        middle = stack_rows(
            *complex_rows(stack_rows(applied_real, applied_imag), inner[e, 0], inner[e, 1])
        )
        again_real, again_imag = complex_rows(middle, inverse[0], inverse[1])
        columns[e] = stack_rows(2.0 * applied_real - again_real, 2.0 * applied_imag - again_imag)

    for e in all_e:
        copies[core_so, e].wait_recv()
        copies[core_so_y, e].wait_recv()
    wide = out.reshape(lines, width)

    def store(buffer, block, which):
        column = pl.multiple_of(which * half + block * LANES, LANES)
        copy = pltpu.make_async_copy(
            buffer.at[block], wide.at[:, pl.ds(column, LANES)], store_sem.at[which, block]
        )
        copy.start()
        return copy

    ident = lax.broadcasted_iota(jnp.int32, (rows, rows), 0) == lax.broadcasted_iota(
        jnp.int32, (rows, rows), 1
    )
    partial = jnp.zeros((1, rows), jnp.float32)
    for e in all_e:
        real, imag = complex_rows(columns[e], right[cluster, e, 0], right[cluster, e, 1])
        scatter(flat, e, 0, get(outer, e, 0, blocks) - real)
        imag = get(outer, e, 1, blocks) - imag
        scatter(flat, e, 1, imag)
        corner = jnp.zeros((rows, rows), jnp.float32)
        for which in range(half // rows):
            chosen = ident & (tile == which)
            corner = corner + jnp.where(chosen, imag[:, which * rows : (which + 1) * rows], 0.0)
        partial = partial + weights[e] * jnp.sum(corner, axis=0, keepdims=True)
    stores = [store(flat, block, cluster) for block in range(blocks)]
    terms[energy] = jnp.broadcast_to(partial, terms.shape[1:])
    swaps = []
    for step in range(1, n_energy):
        swap = pltpu.make_async_remote_copy(
            src_ref=terms.at[energy],
            dst_ref=terms.at[energy],
            send_sem=term_send.at[step],
            recv_sem=term_recv.at[step],
            device_id={"energy": lax.rem(energy + step, n_energy)},
            device_id_type=pl.DeviceIdType.MESH,
        )
        swap.start()
        swaps.append(swap)

    for e in all_e:
        copies[diag, e].wait_recv()
        pass_on(core_diag, e, right_at(over, e, across), to_core)
    pair = 2 * rows
    here = pl.ds(pl.multiple_of(level * pair, pair), pair)
    there = pl.ds(pl.multiple_of((1 - level) * pair, pair), pair)

    def far_part(e, band):
        return complex_rows(
            columns[e, :, band], right[over, e, 0, band, :], right[over, e, 1, band, :]
        )

    for e in all_e:
        copies[core_so_x, e].wait_recv()
        real, imag = far_part(e, here)
        scatter(outer, e, 0, -real)
        scatter(outer, e, 1, -imag)
    for e in all_e:
        copies[core_diag, e].wait_recv()
        real, imag = far_part(e, there)
        scatter(outer, e, 0, get(outer, e, 0) - real)
        scatter(outer, e, 1, get(outer, e, 1) - imag)
    stores += [store(outer, block, over) for block in range(blocks)]
    for swap in swaps:
        swap.wait()
    density[...] = jnp.sum(terms[...], axis=0)[:1]
    for copy in copies.values():
        copy.wait_send()
    for copy in stores:
        copy.wait()


def merge_once(boundary, column_source, energy_weights):
    _, _, rows, energies, _, width = boundary.shape
    half = width // 2
    lines = rows * energies * 2
    n_energy = lax.axis_size("energy")
    n_tile = lax.axis_size("tile")
    bf16, f32 = jnp.bfloat16, jnp.float32
    anywhere = pl.BlockSpec(memory_space=pl.ANY)
    vmem = pl.BlockSpec(memory_space=pltpu.VMEM)
    result, density = pl.pallas_call(
        functools.partial(merge_kernel, n_energy),
        out_shape=(
            jax.ShapeDtypeStruct((rows, energies, 2, width), f32),
            jax.ShapeDtypeStruct((1, rows), f32),
        ),
        in_specs=[anywhere, vmem, pl.BlockSpec(memory_space=pltpu.SMEM)],
        out_specs=(anywhere, vmem),
        scratch_shapes=[
            pltpu.VMEM((2, lines, width), bf16),
            pltpu.VMEM((width, width), bf16),
            pltpu.VMEM((half // LANES, lines, LANES), f32),
            pltpu.VMEM((width // LANES, lines, LANES), f32),
            pltpu.VMEM((energies, 2, rows, half), bf16),
            pltpu.VMEM((energies, 2, rows, half), bf16),
            pltpu.VMEM((energies, 2, half, half), bf16),
            pltpu.VMEM((2, energies, 2, half, half), bf16),
            pltpu.VMEM((2, half, half), bf16),
            pltpu.VMEM((energies, 2 * rows, half), bf16),
            pltpu.VMEM((n_energy, 8, rows), f32),
            pltpu.SemaphoreType.DMA((2,)),
            pltpu.SemaphoreType.DMA((2, half // LANES)),
            pltpu.SemaphoreType.DMA((11, energies)),
            pltpu.SemaphoreType.DMA((11, energies)),
            pltpu.SemaphoreType.DMA((n_energy,)),
            pltpu.SemaphoreType.DMA((n_energy,)),
        ],
        compiler_params=pltpu.CompilerParams(
            collective_id=0, has_side_effects=True, vmem_limit_bytes=48 << 20
        ),
    )(boundary[0], column_source, energy_weights)
    return result[None], density


def solution(mesh):
    placed = (P("cluster", None, "tile", "energy", None, None), P("cluster", None), P("energy"))
    paired = mesh.shape["cluster"] == 2 and mesh.shape["tile"] == 4
    return jax.shard_map(
        merge_once if paired else per_device,
        mesh=mesh,
        in_specs=placed,
        out_specs=(P("cluster", "tile", "energy", None, None), P("cluster", "tile")),
        check_vma=False,
    )
```

```python
import functools

import jax
import jax.numpy as jnp
from jax import lax
from jax.experimental import pallas as pl
from jax.experimental.pallas import tpu as pltpu
from jax.sharding import PartitionSpec as P


def swapped(shard, axis, distance):
    return lax.ppermute(shard, axis, [(i, i ^ 1 << distance) for i in range(lax.axis_size(axis))])


def shortened(shard):
    return jax.tree.map(lambda a: a.astype(jnp.bfloat16) if a.dtype == jnp.float32 else a, shard)


def complex_product(left, right):

    def single(first_part, second_part):
        return jnp.einsum(
            "mek,ken->men", first_part, second_part, preferred_element_type=jnp.float32
        )

    real_part = single(left[:, :, 0], right[:, :, 0]) - single(left[:, :, 1], right[:, :, 1])
    imag_part = single(left[:, :, 0], right[:, :, 1]) + single(left[:, :, 1], right[:, :, 0])
    return jnp.stack([real_part, imag_part], axis=2)


def inverse_guess(interior):
    values = interior.astype(jnp.float32)
    same = jnp.eye(values.shape[0], dtype=jnp.float32)[:, None, None, :]
    diagonal = jnp.sum(values * same, axis=0)
    denom = diagonal[:, 0] * diagonal[:, 0] + diagonal[:, 1] * diagonal[:, 1]
    inv_real = diagonal[:, 0] / denom
    inv_imag = -diagonal[:, 1] / denom
    column_real = inv_real[None, :, :]
    column_imag = inv_imag[None, :, :]
    row_real = inv_real.T[:, :, None]
    row_imag = inv_imag.T[:, :, None]
    values_real = values[:, :, 0]
    values_imag = values[:, :, 1]
    temp_real = values_real * column_real - values_imag * column_imag
    temp_imag = values_real * column_imag + values_imag * column_real
    prod_real = row_real * temp_real - row_imag * temp_imag
    prod_imag = row_real * temp_imag + row_imag * temp_real
    ident = jnp.eye(values.shape[0], dtype=jnp.float32)[:, None, :]
    guess_real = 2.0 * ident * row_real - prod_real
    guess_imag = 2.0 * ident * row_imag - prod_imag
    return jnp.stack([guess_real, guess_imag], axis=2).astype(jnp.bfloat16)


def place_block(block, is_low):
    zeros = jnp.zeros_like(block)
    return jnp.where(
        is_low, jnp.concatenate([block, zeros], axis=3), jnp.concatenate([zeros, block], axis=3)
    )


def swap_separator(separator, level_index):
    return swapped(separator, "cluster", level_index)


def eliminate(outer_coupling, start_block, interior, approx_inverse, coupling_rows):
    applied = complex_product(outer_coupling.astype(jnp.bfloat16), approx_inverse)
    middle = complex_product(applied.astype(jnp.bfloat16), interior).astype(jnp.bfloat16)
    reduced = (2.0 * applied - complex_product(middle, approx_inverse)).astype(jnp.bfloat16)
    row_piece = lax.all_gather(coupling_rows, "tile", axis=0, tiled=True)
    columns = lax.slice_in_dim(reduced, 0, row_piece.shape[0], axis=3)
    return start_block - complex_product(columns, row_piece)


def permuted(stored, source):
    nodes = jnp.arange(stored.shape[-1], dtype=jnp.int32)
    picks = (nodes[:, None] == source[None, :]).astype(jnp.bfloat16)
    picked = jnp.einsum("...j,jm->...m", stored, picks, preferred_element_type=jnp.float32)
    return picked.astype(jnp.bfloat16)


def per_device(boundary, column_source, energy_weights):
    stored = boundary[0]
    canonical = permuted(stored, column_source[0])
    separator = canonical[0]
    outer_rows = canonical[1]
    interior_width = separator.shape[3] // 2
    row_count = separator.shape[0]
    levels = min(2, lax.axis_size("cluster") // 2)
    cluster_index = lax.axis_index("cluster")
    tile_index = lax.axis_index("tile")
    for level_index in range(levels):
        side_bit = cluster_index // 2**level_index % 2
        is_low = side_bit == 0
        final_level = level_index == levels - 1
        if final_level:
            separator = separator.astype(jnp.float32)
            outer_rows = outer_rows.astype(jnp.float32)
            partner_outer = outer_rows
            partner_sep = swap_separator(separator, level_index)
        else:
            partner_sep, partner_outer = (
                swapped(shortened(separator), "cluster", level_index).astype(separator.dtype),
                swapped(shortened(outer_rows), "cluster", level_index).astype(outer_rows.dtype),
            )
            separator = separator.astype(jnp.float32)
            outer_rows = outer_rows.astype(jnp.float32)
            partner_sep = partner_sep.astype(jnp.float32)
            partner_outer = partner_outer.astype(jnp.float32)
        interior_rows = (
            separator[..., :interior_width] + partner_sep[..., :interior_width]
        ).astype(jnp.bfloat16)
        interior = lax.all_gather(interior_rows, "tile", axis=0, tiled=True)
        approx_inverse = inverse_guess(interior)
        low_sep = jnp.where(is_low, separator, partner_sep)
        high_sep = jnp.where(is_low, partner_sep, separator)
        coupling_rows = jnp.concatenate(
            [low_sep[..., interior_width:], high_sep[..., interior_width:]], axis=3
        ).astype(jnp.bfloat16)
        if final_level:
            share = row_count // 2**level_index
            within = cluster_index % 2**level_index
            own_rows = lax.dynamic_slice_in_dim(outer_rows, within * share, share, 0)
            new_rows = eliminate(
                own_rows[..., :interior_width],
                place_block(own_rows[..., interior_width:], is_low),
                interior,
                approx_inverse,
                coupling_rows,
            )
            columns = (
                side_bit * interior_width
                + tile_index * row_count
                + within * share
                + jnp.arange(share, dtype=jnp.int32)
            )
            selector = (
                jnp.arange(new_rows.shape[3], dtype=jnp.int32)[None, :] == columns[:, None]
            ).astype(jnp.float32)
            diagonal = jnp.sum(new_rows[:, :, 1, :] * selector[:, None, :], axis=2)
            partial_sum = jnp.sum(diagonal * energy_weights[None, :], axis=1)
            density = lax.psum(partial_sum, "energy")
            return (new_rows[None], density[None])
        else:
            low_outer = jnp.where(is_low, outer_rows, partner_outer)
            high_outer = jnp.where(is_low, partner_outer, outer_rows)
            outer_coupling = jnp.concatenate(
                [low_outer[..., :interior_width], high_outer[..., :interior_width]], axis=0
            )
            start_block = jnp.concatenate(
                [
                    place_block(low_outer[..., interior_width:], True),
                    place_block(high_outer[..., interior_width:], False),
                ],
                axis=0,
            )
            merged = eliminate(outer_coupling, start_block, interior, approx_inverse, coupling_rows)
            separator = merged[:row_count]
            outer_rows = merged[row_count:]


LANES = 128


def dot(first, second):
    return jnp.dot(first, second, preferred_element_type=jnp.float32)


def complex_rows(stacked, real, imag):
    rows = stacked.shape[0] // 2
    by_real, by_imag = dot(stacked, real), dot(stacked, imag)
    return by_real[:rows] - by_imag[rows:], by_imag[:rows] + by_real[rows:]


def stack_rows(real, imag):
    return jnp.concatenate([real.astype(jnp.bfloat16), imag.astype(jnp.bfloat16)], axis=0)


def guess_of(real, imag):
    size = real.shape[0]
    step = min(128, size)
    ident = (
        lax.broadcasted_iota(jnp.int32, (step, step), 0)
        == lax.broadcasted_iota(jnp.int32, (step, step), 1)
    )

    def inverse_of(axis):
        def diagonal(values):
            cuts = [
                jnp.sum(
                    jnp.where(ident, values[b : b + step, b : b + step], 0.0),
                    axis=axis,
                    keepdims=True,
                )
                for b in range(0, size, step)
            ]
            return jnp.concatenate(cuts, axis=1 - axis)

        diag_real, diag_imag = diagonal(real), diagonal(imag)
        denom = diag_real * diag_real + diag_imag * diag_imag
        return diag_real / denom, -diag_imag / denom

    column_real, column_imag = inverse_of(0)
    row_real, row_imag = inverse_of(1)
    temp_real = real * column_real - imag * column_imag
    temp_imag = real * column_imag + imag * column_real
    prod_real = row_real * temp_real - row_imag * temp_imag
    prod_imag = row_real * temp_imag + row_imag * temp_real
    whole = (
        lax.broadcasted_iota(jnp.int32, real.shape, 0)
        == lax.broadcasted_iota(jnp.int32, real.shape, 1)
    )
    guess_real = jnp.where(whole, 2.0 * row_real, 0.0) - prod_real
    guess_imag = jnp.where(whole, 2.0 * row_imag, 0.0) - prod_imag
    return guess_real.astype(jnp.bfloat16), guess_imag.astype(jnp.bfloat16)


def merge_kernel(
    n_energy,
    boundary,
    source_in,
    weights_in,
    out,
    density,
    source,
    weights,
    raw,
    picks,
    flat,
    outer,
    own_sep,
    peer_sep,
    inner,
    right,
    inverse,
    columns,
    terms,
    load_sem,
    store_sem,
    send_sem,
    recv_sem,
    term_send,
    term_recv,
):
    _, rows, energies, _, width = boundary.shape
    half = width // 2
    lines = rows * energies * 2
    every = energies * 2
    blocks = half // LANES

    def put(buffer, value, first=0):
        for block in range(blocks):
            buffer[first + block] = value[:, block * LANES : (block + 1) * LANES]

    def get(buffer, e, part, first=0):
        line = pl.ds(2 * e + part, rows, stride=every)
        return jnp.concatenate([buffer[first + b, line, :] for b in range(blocks)], axis=1)

    def scatter(buffer, e, part, value):
        line = pl.ds(2 * e + part, rows, stride=every)
        for block in range(blocks):
            buffer[block, line, :] = value[:, block * LANES : (block + 1) * LANES]

    cluster = lax.axis_index("cluster")
    tile = lax.axis_index("tile")
    energy = lax.axis_index("energy")
    over = 1 - cluster
    core = lax.rem(tile, 2)
    level = tile // 2
    beside = level * 2 + (1 - core)
    across = (1 - level) * 2 + core
    to_x, to_y, to_core = {"cluster": over}, {"tile": across}, {"tile": beside}

    loads = [
        pltpu.make_async_copy(
            boundary.at[part].reshape(lines, width), raw.at[part], load_sem.at[part]
        )
        for part in range(2)
    ]
    loads.insert(0, pltpu.make_async_copy(source_in, source, load_sem.at[2]))
    loads.append(pltpu.make_async_copy(weights_in, weights, load_sem.at[3]))
    for load in loads:
        load.start()
    barrier = pltpu.get_barrier_semaphore()
    for there in (to_x, to_y, to_core):
        pl.semaphore_signal(barrier, inc=1, device_id=there, device_id_type=pl.DeviceIdType.MESH)
    for step in range(1, n_energy):
        pl.semaphore_signal(
            barrier,
            inc=1,
            device_id={"energy": lax.rem(energy + step, n_energy)},
            device_id_type=pl.DeviceIdType.MESH,
        )

    loads[0].wait()
    wanted = source[...]
    deep = min(256, width)
    for begin in range(0, width, deep):
        node = lax.broadcasted_iota(jnp.int32, (deep, width), 0) + begin
        picks[begin : begin + deep, :] = jnp.where(node == wanted, 1.0, 0.0).astype(jnp.bfloat16)
    loads[1].wait()
    pl.semaphore_wait(barrier, 2 + n_energy)

    def rows_of(which):
        return pl.ds(pl.multiple_of(which * rows, rows), rows)

    def send(kind, e, src, dst, there):
        copy = pltpu.make_async_remote_copy(
            src_ref=src,
            dst_ref=dst,
            send_sem=send_sem.at[kind, e],
            recv_sem=recv_sem.at[kind, e],
            device_id=there,
            device_id_type=pl.DeviceIdType.MESH,
        )
        copy.start()
        copies[kind, e] = copy

    def pass_on(kind, e, ref, there):
        send(kind, e, ref, ref, there)

    def right_at(which, e, block):
        return right.at[which, e, :, rows_of(block), :]

    def inner_at(e, block):
        return inner.at[e, :, rows_of(block), :]

    copies = {}
    sep_x, so_x, so_y, in_y, diag = range(5)
    core_in, core_in_y, core_so, core_so_y, core_so_x, core_diag = range(5, 11)
    all_e = list(range(energies))
    by_x = energies // 2

    put(flat, dot(raw[0], picks[:, :half]))
    for e in all_e:
        for part in range(2):
            own_sep[e, part] = get(flat, e, part).astype(jnp.bfloat16)
        send(sep_x, e, own_sep.at[e], peer_sep.at[e], to_x)
    put(flat, dot(raw[0], picks[:, half:]))
    for e in all_e:
        for part in range(2):
            right[cluster, e, part, rows_of(tile), :] = get(flat, e, part).astype(jnp.bfloat16)
        pass_on(so_y, e, right_at(cluster, e, tile), to_y)
    for e in reversed(all_e):
        pass_on(so_x, e, right_at(cluster, e, tile), to_x)
    for e in all_e:
        pass_on(core_so, e, right_at(cluster, e, tile), to_core)

    loads[2].wait()
    loads[3].wait()
    put(outer, dot(raw[1], picks[:, :half]))
    put(outer, dot(raw[1], picks[:, half:]), blocks)

    for e in all_e:
        copies[sep_x, e].wait_recv()
        for part in range(2):
            inner[e, part, rows_of(tile), :] = (
                own_sep[e, part].astype(jnp.float32) + peer_sep[e, part].astype(jnp.float32)
            ).astype(jnp.bfloat16)
        pass_on(in_y, e, inner_at(e, tile), to_y)
        pass_on(core_in, e, inner_at(e, tile), to_core)
        copies[so_y, e].wait_recv()
        if e < by_x:
            pass_on(diag, e, right_at(cluster, e, across), to_x)
        pass_on(core_so_y, e, right_at(cluster, e, across), to_core)

    def take_x(e):
        copies[so_x, e].wait_recv()
        if e >= by_x:
            pass_on(diag, e, right_at(over, e, tile), to_y)
        pass_on(core_so_x, e, right_at(over, e, tile), to_core)

    def take_inner(e):
        copies[in_y, e].wait_recv()
        pass_on(core_in_y, e, inner_at(e, across), to_core)

    for e, x in zip(all_e, reversed(all_e)):
        take_inner(e)
        take_x(x)
        copies[core_in, e].wait_recv()
        copies[core_in_y, e].wait_recv()
        guess_real, guess_imag = guess_of(
            inner[e, 0].astype(jnp.float32), inner[e, 1].astype(jnp.float32)
        )
        inverse[0] = guess_real
        inverse[1] = guess_imag
        left = stack_rows(get(outer, e, 0), get(outer, e, 1))
        applied_real, applied_imag = complex_rows(left, inverse[0], inverse[1])
        middle = stack_rows(
            *complex_rows(stack_rows(applied_real, applied_imag), inner[e, 0], inner[e, 1])
        )
        again_real, again_imag = complex_rows(middle, inverse[0], inverse[1])
        columns[e] = stack_rows(2.0 * applied_real - again_real, 2.0 * applied_imag - again_imag)

    for e in all_e:
        copies[core_so, e].wait_recv()
        copies[core_so_y, e].wait_recv()
    wide = out.reshape(lines, width)

    def store(buffer, block, which):
        column = pl.multiple_of(which * half + block * LANES, LANES)
        copy = pltpu.make_async_copy(
            buffer.at[block], wide.at[:, pl.ds(column, LANES)], store_sem.at[which, block]
        )
        copy.start()
        return copy

    ident = lax.broadcasted_iota(jnp.int32, (rows, rows), 0) == lax.broadcasted_iota(
        jnp.int32, (rows, rows), 1
    )
    partial = jnp.zeros((1, rows), jnp.float32)
    for e in all_e:
        real, imag = complex_rows(columns[e], right[cluster, e, 0], right[cluster, e, 1])
        scatter(flat, e, 0, get(outer, e, 0, blocks) - real)
        imag = get(outer, e, 1, blocks) - imag
        scatter(flat, e, 1, imag)
        corner = jnp.zeros((rows, rows), jnp.float32)
        for which in range(half // rows):
            chosen = ident & (tile == which)
            corner = corner + jnp.where(chosen, imag[:, which * rows : (which + 1) * rows], 0.0)
        partial = partial + weights[e] * jnp.sum(corner, axis=0, keepdims=True)
    stores = [store(flat, block, cluster) for block in range(blocks)]
    terms[energy] = jnp.broadcast_to(partial, terms.shape[1:])
    swaps = []
    for step in range(1, n_energy):
        swap = pltpu.make_async_remote_copy(
            src_ref=terms.at[energy],
            dst_ref=terms.at[energy],
            send_sem=term_send.at[step],
            recv_sem=term_recv.at[step],
            device_id={"energy": lax.rem(energy + step, n_energy)},
            device_id_type=pl.DeviceIdType.MESH,
        )
        swap.start()
        swaps.append(swap)

    for e in all_e:
        copies[diag, e].wait_recv()
        pass_on(core_diag, e, right_at(over, e, across), to_core)
    pair = 2 * rows
    here = pl.ds(pl.multiple_of(level * pair, pair), pair)
    there = pl.ds(pl.multiple_of((1 - level) * pair, pair), pair)

    def far_part(e, band):
        return complex_rows(
            columns[e, :, band], right[over, e, 0, band, :], right[over, e, 1, band, :]
        )

    for e in all_e:
        copies[core_so_x, e].wait_recv()
        real, imag = far_part(e, here)
        scatter(outer, e, 0, -real)
        scatter(outer, e, 1, -imag)
    for e in all_e:
        copies[core_diag, e].wait_recv()
        real, imag = far_part(e, there)
        scatter(outer, e, 0, get(outer, e, 0) - real)
        scatter(outer, e, 1, get(outer, e, 1) - imag)
    stores += [store(outer, block, over) for block in range(blocks)]
    for swap in swaps:
        swap.wait()
    density[...] = jnp.sum(terms[...], axis=0)[:1]
    for copy in copies.values():
        copy.wait_send()
    for copy in stores:
        copy.wait()


def merge_once(boundary, column_source, energy_weights):
    _, _, rows, energies, _, width = boundary.shape
    half = width // 2
    lines = rows * energies * 2
    n_energy = lax.axis_size("energy")
    n_tile = lax.axis_size("tile")
    bf16, f32 = jnp.bfloat16, jnp.float32
    anywhere = pl.BlockSpec(memory_space=pl.ANY)
    vmem = pl.BlockSpec(memory_space=pltpu.VMEM)
    result, density = pl.pallas_call(
        functools.partial(merge_kernel, n_energy),
        out_shape=(
            jax.ShapeDtypeStruct((rows, energies, 2, width), f32),
            jax.ShapeDtypeStruct((1, rows), f32),
        ),
        in_specs=[pl.BlockSpec(memory_space=pltpu.HBM)] * 3,
        out_specs=(anywhere, vmem),
        scratch_shapes=[
            pltpu.VMEM(column_source.shape, jnp.int32),
            pltpu.SMEM(energy_weights.shape, f32),
            pltpu.VMEM((2, lines, width), bf16),
            pltpu.VMEM((width, width), bf16),
            pltpu.VMEM((half // LANES, lines, LANES), f32),
            pltpu.VMEM((width // LANES, lines, LANES), f32),
            pltpu.VMEM((energies, 2, rows, half), bf16),
            pltpu.VMEM((energies, 2, rows, half), bf16),
            pltpu.VMEM((energies, 2, half, half), bf16),
            pltpu.VMEM((2, energies, 2, half, half), bf16),
            pltpu.VMEM((2, half, half), bf16),
            pltpu.VMEM((energies, 2 * rows, half), bf16),
            pltpu.VMEM((n_energy, 8, rows), f32),
            pltpu.SemaphoreType.DMA((4,)),
            pltpu.SemaphoreType.DMA((2, half // LANES)),
            pltpu.SemaphoreType.DMA((11, energies)),
            pltpu.SemaphoreType.DMA((11, energies)),
            pltpu.SemaphoreType.DMA((n_energy,)),
            pltpu.SemaphoreType.DMA((n_energy,)),
        ],
        compiler_params=pltpu.CompilerParams(
            collective_id=0, has_side_effects=True, vmem_limit_bytes=62 << 20
        ),
    )(boundary[0], column_source, energy_weights)
    return result[None], density


def solution(mesh):
    placed = (P("cluster", None, "tile", "energy", None, None), P("cluster", None), P("energy"))
    paired = mesh.shape["cluster"] == 2 and mesh.shape["tile"] == 4
    return jax.shard_map(
        merge_once if paired else per_device,
        mesh=mesh,
        in_specs=placed,
        out_specs=(P("cluster", "tile", "energy", None, None), P("cluster", "tile")),
        check_vma=False,
    )
```
